32 devices in a mesh: fsdp: 8 (over z, core), seq: 4 (over y, x).
Axes of the slice: x: 2, y: 2, z: 4, core: 2. Of those that a mesh axis runs over, the one named last changes fastest.
Arguments:
- hidden_in: bfloat16 [32, 5, 1536], P('fsdp'), may hold values from -6 to 6
- norm_gain: float32 [1536], replicated, may hold values from 0.1 to 1.9
- w_qkv: bfloat16 [1536, 3, 24, 64], P(None, None, 'seq', 'fsdp'), may hold values from -0.15625 to 0.15625
- w_forget: bfloat16 [1536, 24], replicated, may hold values from -0.15625 to 0.15625
- forget_bias: float32 [24], replicated, may hold values from 1 to 5
- cache_keys: bfloat16 [32, 2048, 1536], P('fsdp', 'seq')
- cache_values: bfloat16 [32, 2048, 1536], P('fsdp', 'seq'), may hold values from -6 to 6
- cache_forget: float32 [32, 24, 2048], P('fsdp', None, 'seq')
- cache_lengths: int32 [32], P('fsdp'), may hold values from 128 to 2048, as said below
- piece_map: int32 [32, 4], P('fsdp'), may hold values from 0 to 3, each once within a row
- draft_counts: int32 [32], P('fsdp'), may hold values from 1 to 4
Outputs:
- verified: bfloat16 [32, 5, 1536], P('fsdp', None, 'seq')
The draws below stay inside these ranges and needn't reach their ends.
Inputs may be any that keep to these rules, and one draw needn't show every extreme that they name: `cache_lengths`: 8 requests drawn at random have lengths from 1793 to 2048, one exactly 2048; the others have lengths from 128 to 256, one exactly 128.
All inputs are finite; a program needn't handle non-finite values.
Results may differ from the reference program's by a relative error of at most 0.012.
The reference program's roundings to bfloat16 on the way count: a program that leaves them out, or rounds other values in their place, can miss the bound.
Values may be sent and summed in bfloat16 or wider, within the bound.
A program may use at most 128 MiB of HBM per device.

```python
import math
import jax
import jax.numpy as jnp
from jax import lax

D = 1536
HEAD_TOTAL = 24
HEAD_DIM = 64
DRAFT = 4
NEW = 5
PIECE_POSITIONS = 512
REQUEST_TOTAL = 32
CACHE_POSITIONS = 2048
N_SEQ = 4


def draw_cache_keys(key, part):
    earlier = jax.random.fold_in(key, 0)
    inner_width = HEAD_TOTAL * HEAD_DIM
    table_entries = jax.random.normal(earlier, (REQUEST_TOTAL, N_SEQ, PIECE_POSITIONS, inner_width), jnp.float32)
    return table_entries.reshape(REQUEST_TOTAL, CACHE_POSITIONS, inner_width).astype(jnp.bfloat16)


def draw_cache_forget(key, part):
    random_subkeys = jax.random.split(key, 5)
    rate_low = math.log(1.0 / (16.0 * CACHE_POSITIONS))
    rate_high = math.log(1.0 / 30.0)
    forget_decay = jnp.exp(jax.random.uniform(random_subkeys[0], (REQUEST_TOTAL, HEAD_TOTAL, 1, 1), jnp.float32, rate_low, rate_high))
    device_multiplier = jnp.exp(jax.random.uniform(random_subkeys[1], (REQUEST_TOTAL, HEAD_TOTAL, N_SEQ, 1), jnp.float32, math.log(0.5), math.log(2.0)))
    random_noise = jax.random.uniform(random_subkeys[2], (REQUEST_TOTAL, HEAD_TOTAL, N_SEQ, PIECE_POSITIONS), jnp.float32, 0.5, 1.5)
    spike_events = jax.random.bernoulli(random_subkeys[3], 3.0 / CACHE_POSITIONS, (REQUEST_TOTAL, HEAD_TOTAL, N_SEQ, PIECE_POSITIONS))
    spike_penalty = jax.random.uniform(random_subkeys[4], (REQUEST_TOTAL, HEAD_TOTAL, N_SEQ, PIECE_POSITIONS), jnp.float32, 0.2, 0.5)
    table_entries = -forget_decay * device_multiplier * random_noise + jnp.where(spike_events, jnp.log1p(-spike_penalty), 0.0)
    return table_entries.reshape(REQUEST_TOTAL, HEAD_TOTAL, CACHE_POSITIONS).astype(jnp.float32)


def draw_cache_lengths(key, part):
    earlier, second, third = jax.random.split(key, 3)
    request_rank = jax.random.permutation(earlier, REQUEST_TOTAL)
    long_len = CACHE_POSITIONS - jax.random.randint(second, (REQUEST_TOTAL,), 0, PIECE_POSITIONS // 2)
    short_len = jax.random.randint(third, (REQUEST_TOTAL,), PIECE_POSITIONS // 4, PIECE_POSITIONS // 2 + 1)
    lengths = jnp.where(request_rank == 0, CACHE_POSITIONS, jnp.where(request_rank < REQUEST_TOTAL // 4, long_len, jnp.where(request_rank == REQUEST_TOTAL // 4, PIECE_POSITIONS // 4, short_len)))
    return lengths.astype(jnp.int32)


def touch_ends(drawn, own_key, smallest, high):
    shape = drawn.shape
    index_at = [jax.random.randint(jax.random.fold_in(own_key, axis), (), 0, shape[axis]) for axis in range(len(shape))]
    drawn = drawn.at[tuple(index_at)].set(smallest)
    longest = shape.index(max(shape))
    index_at[longest] = (index_at[longest] + 1) % shape[longest]
    return drawn.at[tuple(index_at)].set(high)


def shard_levels(rng, shape, shards, low, high):
    level = 1.0
    for axis_at, shards_of in shards:
        steps = jax.random.uniform(jax.random.fold_in(jax.random.fold_in(rng, 6), axis_at), (shards_of,), jnp.float32, low / len(shards), high / len(shards))
        level = level * jnp.repeat(jnp.exp(steps), shape[axis_at] // shards_of).reshape((-1,) + (1,) * (len(shape) - 1 - axis_at))
    return level


def gaussian(rng, shape, spread, bound, shards=(), kind=jnp.bfloat16):
    entries = jax.random.normal(rng, shape, jnp.float32) * spread
    if len(shards) > 0:
        entries = shard_levels(rng, shape, shards, -0.22, 0.18) * entries
    return jnp.clip(entries, min=-bound, max=bound).astype(kind)


def setup_inputs(seed: int = 0) -> dict:
    splits = jax.random.split(jax.random.key(seed), 12)
    hidden_in = gaussian(splits[0], (REQUEST_TOTAL, NEW, D), 1.0, 6.0, ((0, 8),))
    norm_gain = jnp.clip(1.0 + 0.18 * jax.random.normal(splits[1], (D,), jnp.float32), 0.1, 1.9)
    w_qkv = gaussian(splits[2], (D, 3, HEAD_TOTAL, HEAD_DIM), D ** -0.5, 0.15625, ((2, 4), (3, 8)))
    w_forget = gaussian(splits[3], (D, HEAD_TOTAL), D ** -0.5, 0.15625)
    forget_bias = jnp.clip(jax.random.uniform(splits[4], (HEAD_TOTAL,), jnp.float32, 1.0, 5.0), 1.0, 5.0)
    cache_keys = draw_cache_keys(jax.random.fold_in(splits[11], 71), 0)
    cache_values = gaussian(splits[6], (REQUEST_TOTAL, CACHE_POSITIONS, HEAD_TOTAL * HEAD_DIM), 1.0, 6.0, ((0, 8), (1, 4)))
    cache_forget = draw_cache_forget(jax.random.fold_in(splits[11], 71), 0)
    cache_lengths = draw_cache_lengths(jax.random.fold_in(splits[11], 71), 0)
    piece_map = jax.vmap(lambda own: jax.random.permutation(own, N_SEQ))(jax.random.split(splits[9], REQUEST_TOTAL)).reshape((REQUEST_TOTAL, N_SEQ)).astype(jnp.int32)
    draft_counts = touch_ends(jax.random.randint(splits[10], (REQUEST_TOTAL,), 1, DRAFT + 1), jax.random.fold_in(splits[10], 1), 1, DRAFT).astype(jnp.int32)
    return {"hidden_in": hidden_in, "norm_gain": norm_gain, "w_qkv": w_qkv, "w_forget": w_forget, "forget_bias": forget_bias, "cache_keys": cache_keys, "cache_values": cache_values, "cache_forget": cache_forget, "cache_lengths": cache_lengths, "piece_map": piece_map, "draft_counts": draft_counts}


norm_eps = 1e-06
neg_fill = -1e+30

def normalize(rows, gain):
    values = rows.astype(jnp.float32)
    mean_sq = lax.optimization_barrier(jnp.mean(values * values, axis=-1, keepdims=True))
    return (values * lax.rsqrt(mean_sq + norm_eps) * gain).astype(jnp.bfloat16)

def reference(hidden_in, norm_gain, w_qkv, w_forget, forget_bias, cache_keys, cache_values, cache_forget, cache_lengths, piece_map, draft_counts):
    inner_width = HEAD_TOTAL * HEAD_DIM
    normed = normalize(hidden_in, norm_gain).reshape(REQUEST_TOTAL * NEW, D)
    projected = jnp.dot(normed, w_qkv.reshape(D, 3 * inner_width), preferred_element_type=jnp.float32).astype(jnp.bfloat16)
    projected = projected.reshape(REQUEST_TOTAL, NEW, 3, HEAD_TOTAL, HEAD_DIM)
    gate_logit = jnp.dot(normed, w_forget, preferred_element_type=jnp.float32).reshape(REQUEST_TOTAL, NEW, HEAD_TOTAL) + forget_bias
    prefix = jnp.cumsum(jax.nn.log_sigmoid(gate_logit), axis=1)
    logit_scale = HEAD_DIM ** (-0.5)
    step_ids = jnp.arange(NEW, dtype=jnp.int32)
    causal = step_ids[None, :] <= step_ids[:, None]

    def per_request(request_items):
        projected_row, prefix_row, key_rows, value_rows, forget_rows, length, piece_order, draft_count = request_items
        query_rows_all = projected_row[:, 0].astype(jnp.float32)
        fresh_keys = projected_row[:, 1].astype(jnp.float32)
        fresh_values = projected_row[:, 2].astype(jnp.float32)
        key_history = key_rows.reshape(N_SEQ, PIECE_POSITIONS, inner_width)[piece_order].reshape(CACHE_POSITIONS, HEAD_TOTAL, HEAD_DIM).astype(jnp.float32)
        value_history = value_rows.reshape(N_SEQ, PIECE_POSITIONS, inner_width)[piece_order].reshape(CACHE_POSITIONS, HEAD_TOTAL, HEAD_DIM).astype(jnp.float32)
        forget_log = forget_rows.reshape(HEAD_TOTAL, N_SEQ, PIECE_POSITIONS)[:, piece_order].reshape(HEAD_TOTAL, CACHE_POSITIONS)
        live_mask = jnp.arange(CACHE_POSITIONS, dtype=jnp.int32) < length
        masked = jnp.where(live_mask[None, :], forget_log, 0.0)
        trailing_part = lax.optimization_barrier(jnp.sum(masked, axis=-1, keepdims=True)) - jnp.cumsum(masked, axis=-1)
        prefix_transposed = prefix_row.T
        cache_logits = jnp.einsum('cuv,kuv->uck', query_rows_all, key_history) * logit_scale + trailing_part[:, None, :] + prefix_transposed[:, :, None]
        fresh_logits = jnp.einsum('ufq,lfq->ful', query_rows_all, fresh_keys) * logit_scale + prefix_transposed[:, :, None] - prefix_transposed[:, None, :]
        cache_logits = jnp.where(live_mask[None, None, :], cache_logits, neg_fill)
        fresh_logits = jnp.where(causal[None], fresh_logits, neg_fill)
        row_max = jnp.maximum(lax.optimization_barrier(jnp.max(cache_logits, axis=-1)), lax.optimization_barrier(jnp.max(fresh_logits, axis=-1)))
        cache_weights = jnp.where(live_mask[None, None, :], jnp.exp(cache_logits - row_max[..., None]), 0.0)
        new_weights = jnp.where(causal[None], jnp.exp(fresh_logits - row_max[..., None]), 0.0)
        total_sum = lax.optimization_barrier(jnp.sum(cache_weights, axis=-1)) + lax.optimization_barrier(jnp.sum(new_weights, axis=-1))
        cache_rounded = lax.optimization_barrier(cache_weights.astype(jnp.bfloat16)).astype(jnp.float32)
        fresh_rounded = lax.optimization_barrier(new_weights.astype(jnp.bfloat16)).astype(jnp.float32)
        blend_weights = jnp.einsum('slb,bsf->slf', cache_rounded, value_history) + jnp.einsum('zyv,vzs->zys', fresh_rounded, fresh_values)
        result = blend_weights / total_sum[..., None]
        live_rows = step_ids <= draft_count
        result = jnp.where(live_rows[None, :, None], result, 0.0)
        return jnp.transpose(result, (1, 0, 2)).reshape(NEW, inner_width).astype(jnp.bfloat16)
    return lax.map(per_request, (projected, prefix, cache_keys, cache_values, cache_forget, cache_lengths, piece_map, draft_counts))
```

```python
import functools

import jax
import jax.numpy as jnp
import numpy as np
from jax import lax
from jax.experimental import pallas as pl
from jax.experimental.pallas import tpu as pltpu
from jax.sharding import PartitionSpec as P

HEAD_DIM = 64
ROWS = 8
SPLIT = 4
TILE = 256
norm_eps = 1e-06
neg_fill = -1e30
f32 = jnp.float32
bf16 = jnp.bfloat16
NT = (((1,), (1,)), ((), ()))


def dot_nt(a, b):
    return lax.dot_general(a, b, NT, preferred_element_type=f32)


def dot_exact(a, ones):
    hi = a.astype(bf16)
    rest = a - hi.astype(f32)
    mid = rest.astype(bf16)
    low = (rest - mid.astype(f32)).astype(bf16)
    n = a.shape[0]
    if n % 16 == 0:
        out = jnp.dot(jnp.concatenate([hi, mid, low], axis=0), ones, preferred_element_type=f32)
        return out[:n] + out[n : 2 * n] + out[2 * n :]
    return sum(jnp.dot(x, ones, preferred_element_type=f32) for x in (hi, mid, low))


def iota(shape, dim):
    return lax.broadcasted_iota(jnp.int32, shape, dim)


def kernel(
    cfg,
    lens, pmap, drafts, hidden, gain, wf, bias, w, perm, kc, vc, fg,
    out,
    wbuf, xs, nf, ysend, yrecv, qall, qf, kown, vown, kv_k, kv_v, permv, fgv, suf, pre, acc,
    asend, arecv, ssend, srecv,
    lsem, wsend, wrecv, s1, r1, s2, r2, s3, r3, s4, r4, s5, r5, s6, r6,
):
    n_half, n_seq, reqs, new, own, rp = cfg
    head_count = wf.shape[0]
    width = hidden.shape[2]
    part = width // SPLIT
    own_width = own * HEAD_DIM
    piece_len = kc.shape[1]
    rows = reqs * ROWS
    me_f = lax.axis_index("fsdp")
    me_s = lax.axis_index("seq")
    me_z = me_f // 2
    me_c = me_f % 2
    sib = me_z * 2 + 1 - me_c
    me_q = me_s % SPLIT
    block = me_s - me_q

    local = [
        pltpu.make_async_copy(fg, fgv, lsem.at[0]),
        pltpu.make_async_copy(perm, permv, lsem.at[1]),
    ]
    wrow = [pl.ds(pl.multiple_of(p * 128 + me_c * rp, 16), rp) for p in range(3)]
    wlocal = [pltpu.make_async_copy(w.at[p], wbuf.at[wrow[p]], lsem.at[2 + p]) for p in range(3)]
    big = []
    for r in range(reqs):
        big.append(pltpu.make_async_copy(kc.at[r], kv_k.at[r], lsem.at[5 + r]))
    for r in range(reqs):
        big.append(pltpu.make_async_copy(vc.at[r], kv_v.at[r], lsem.at[5 + reqs + r]))

    barrier = pltpu.get_barrier_semaphore()
    MESH = pl.DeviceIdType.MESH
    for j in range(1, n_half):
        pl.semaphore_signal(barrier, 1, device_id={"fsdp": (me_z + j) % n_half * 2 + me_c}, device_id_type=MESH)
    for j in range(1, n_seq):
        pl.semaphore_signal(barrier, 1, device_id={"seq": (me_s + j) % n_seq}, device_id_type=MESH)
    pl.semaphore_signal(barrier, 1, device_id={"fsdp": sib}, device_id_type=MESH)
    for c in wlocal + local + big:
        c.start()

    nf[...] = jnp.zeros_like(nf)
    for m in range(new):
        x = hidden[m].astype(f32)
        mean_sq = jnp.mean(x * x, axis=-1, keepdims=True)
        x = x * lax.rsqrt(mean_sq + norm_eps) * gain[...]
        for r in range(reqs):
            nf[r * ROWS + m : r * ROWS + m + 1, :] = x[r : r + 1]
    normed = nf[...].astype(bf16)
    for q in range(SPLIT):
        xs[me_z, q] = normed[:, q * part : (q + 1) * part]
    if 2 * rp < 128:
        for p in range(3):
            wbuf[p * 128 + 2 * rp : (p + 1) * 128, :] = jnp.zeros((128 - 2 * rp, width), bf16)

    pl.semaphore_wait(barrier, n_half + n_seq - 1)

    sends = []
    first = []
    for j in range(1, n_half):
        peer = (me_z + j) % n_half
        c = pltpu.make_async_remote_copy(
            xs.at[me_z, me_q], xs.at[me_z, me_q], s1.at[peer], r1.at[me_z],
            device_id={"fsdp": peer * 2 + me_c}, device_id_type=MESH,
        )
        c.start()
        sends.append(c)
    for p in range(3):
        c = pltpu.make_async_remote_copy(
            w.at[p], wbuf.at[wrow[p]], wsend.at[p], wrecv.at[p],
            device_id={"fsdp": sib}, device_id_type=MESH,
        )
        c.start()
        sends.append(c)

    local[0].wait()
    lane = iota((1, piece_len), 1)

    def limit_of(r):
        slot = jnp.int32(0)
        for p in range(n_seq):
            slot = slot + jnp.where(pmap[r * n_seq + p] == me_s, p, 0)
        return lens[r] - slot * piece_len

    for r in range(reqs):
        fgv[r] = jnp.where(lane < limit_of(r), fgv[r], 0.0)
    after = (iota((piece_len, piece_len), 0) > iota((piece_len, piece_len), 1)).astype(bf16)
    masked = jnp.concatenate([fgv[r] for r in range(reqs)], axis=0)
    trailing = dot_exact(masked, after)
    for r in range(reqs):
        suf[r] = trailing[r * head_count : (r + 1) * head_count]

    gate = dot_nt(wf[...], normed) + bias[...]
    gate = jnp.minimum(gate, 0.0) - jnp.log(1.0 + jnp.exp(-jnp.abs(gate)))
    ir, ic = iota((rows, rows), 0), iota((rows, rows), 1)
    upto = ((ir >> 3 == ic >> 3) & (ir <= ic)).astype(bf16)
    pre[...] = dot_exact(gate, upto)

    for j in range(n_half):
        src = (me_z + j) % n_half
        if j:
            pltpu.make_async_remote_copy(
                xs.at[src, me_q], xs.at[src, me_q], s1.at[src], r1.at[src],
                device_id={"fsdp": src * 2 + me_c}, device_id_type=MESH,
            ).wait_recv()
            for i in range(1, SPLIT):
                to = (me_q + i) % SPLIT
                c = pltpu.make_async_remote_copy(
                    xs.at[src, me_q], xs.at[src, me_q], s2.at[src * SPLIT + to], r2.at[src * SPLIT + me_q],
                    device_id={"seq": block + to}, device_id_type=MESH,
                )
                c.start()
                sends.append(c)
    for c in wlocal:
        c.wait()
    for c in sends[n_half - 1 : n_half + 2]:
        c.wait_recv()
    for j in range(1, n_half):
        src = (me_z + j) % n_half
        for i in range(1, SPLIT):
            q = (me_q + i) % SPLIT
            pltpu.make_async_remote_copy(
                xs.at[src, q], xs.at[src, q], s2.at[src * SPLIT + q], r2.at[src * SPLIT + q],
                device_id={"seq": block + q}, device_id_type=MESH,
            ).wait_recv()

    total = jnp.zeros((n_half * rows, 384), f32)
    for q in range(SPLIT):
        x = jnp.concatenate([xs[z, q] for z in range(n_half)], axis=0)
        total = total + dot_nt(x, wbuf[:, q * part : (q + 1) * part])
    proj = total.astype(bf16)
    for z in range(n_half):
        for p in range(3):
            ysend[z, p] = proj[z * rows : (z + 1) * rows, p * 128 : (p + 1) * 128]
    for j in range(1, n_half):
        peer = (me_z + j) % n_half
        c = pltpu.make_async_remote_copy(
            ysend.at[peer], yrecv.at[me_z], s3.at[peer], r3.at[me_z],
            device_id={"fsdp": peer * 2 + me_c}, device_id_type=MESH,
        )
        c.start()
        sends.append(c)
    yrecv[me_z] = ysend[me_z]
    local[1].wait()
    for j in range(1, n_half):
        src = (me_z + j) % n_half
        pltpu.make_async_remote_copy(
            ysend.at[src], yrecv.at[src], s3.at[src], r3.at[src],
            device_id={"fsdp": src * 2 + me_c}, device_id_type=MESH,
        ).wait_recv()
    y = jnp.concatenate(
        [jnp.concatenate([yrecv[z, p] for z in range(n_half)], axis=1) for p in range(3)], axis=0
    )
    qkv = jnp.dot(y, permv[...], preferred_element_type=f32).astype(bf16)
    qall[me_s] = qkv[:rows]
    kown[...] = qkv[rows : 2 * rows]
    vown[...] = qkv[2 * rows :]
    for j in range(1, n_seq):
        peer = (me_s + j) % n_seq
        c = pltpu.make_async_remote_copy(
            qall.at[me_s], qall.at[me_s], s4.at[peer], r4.at[me_s],
            device_id={"seq": peer}, device_id_type=MESH,
        )
        c.start()
        sends.append(c)
    for j in range(1, n_seq):
        src = (me_s + j) % n_seq
        pltpu.make_async_remote_copy(
            qall.at[src], qall.at[src], s4.at[src], r4.at[src],
            device_id={"seq": src}, device_id_type=MESH,
        ).wait_recv()
    qf[...] = jnp.concatenate([qall[s].astype(f32) for s in range(n_seq)], axis=1) * (HEAD_DIM**-0.5)

    for c in big:
        c.wait()

    lane_head = iota((ROWS, TILE), 1) >> 6
    stat_lane = iota((ROWS, 128), 1)
    per = TILE // HEAD_DIM

    def request(r, carry):
        at = pl.ds(pl.multiple_of(r * ROWS, ROWS), ROWS)
        live = lane < limit_of(r)
        stats = [jnp.zeros((ROWS, 128), f32) for _ in range(n_seq)]
        for g in range(width // TILE):
            cols = slice(g * TILE, (g + 1) * TILE)
            heads = slice(g * per, (g + 1) * per)
            q = qf[at, cols]
            qb = jnp.concatenate([jnp.where(lane_head == h, q, 0.0) for h in range(per)], axis=0).astype(bf16)
            sc = dot_nt(qb, kv_k[r, :, cols])
            trail = suf[r, heads, :]
            sc = sc + jnp.broadcast_to(trail[:, None, :], (per, ROWS, piece_len)).reshape(per * ROWS, piece_len)
            sc = jnp.where(live, sc, neg_fill)
            top = jnp.max(sc, axis=-1, keepdims=True)
            wt = jnp.where(live, jnp.exp(sc - top), 0.0)
            sums = jnp.sum(wt, axis=-1, keepdims=True)
            av = jnp.dot(wt.astype(bf16), kv_v[r, :, cols], preferred_element_type=f32)
            got = jnp.zeros((ROWS, TILE), f32)
            piece_sum = jnp.sum(fgv[r, heads, :], axis=-1, keepdims=True)
            for h in range(per):
                hr = slice(h * ROWS, (h + 1) * ROWS)
                got = jnp.where(lane_head == h, av[hr], got)
                s, hl = divmod(g * per + h, own)
                t = jnp.where(stat_lane == hl, top[hr], stats[s])
                t = jnp.where(stat_lane == 32 + hl, sums[hr], t)
                stats[s] = jnp.where(stat_lane == 64 + hl, piece_sum[h : h + 1], t)
            acc[at, cols] = got
        for s in range(n_seq):
            ssend[s, at, :] = stats[s]
        return carry

    lax.fori_loop(0, reqs, request, 0)
    for s in range(n_seq):
        asend[s] = acc[:, s * own_width : (s + 1) * own_width].astype(bf16)
    for j in range(1, n_seq):
        peer = (me_s + j) % n_seq
        for c in (
            pltpu.make_async_remote_copy(
                ssend.at[peer], srecv.at[me_s], s5.at[peer], r5.at[me_s],
                device_id={"seq": peer}, device_id_type=MESH,
            ),
            pltpu.make_async_remote_copy(
                asend.at[peer], arecv.at[me_s], s6.at[peer], r6.at[me_s],
                device_id={"seq": peer}, device_id_type=MESH,
            ),
        ):
            c.start()
            sends.append(c)
    arecv[me_s] = asend[me_s]
    srecv[me_s] = ssend[me_s]

    own_lane = iota((rows, own_width), 1) >> 6
    qo = qall[me_s].astype(f32) * (HEAD_DIM**-0.5)
    qb = jnp.concatenate([jnp.where(own_lane == h, qo, 0.0) for h in range(own)], axis=0).astype(bf16)
    fresh = dot_nt(qb, kown[...])
    ok = (ir >> 3 == ic >> 3) & (ic & 7 <= ir & 7) & (ic & 7 < new)
    wide = iota((rows, 128), 1)
    f_max = jnp.zeros((rows, 128), f32)
    f_sum = jnp.zeros((rows, 128), f32)
    weights = []
    for h in range(own):
        sc = fresh[h * rows : (h + 1) * rows] - pre[pl.ds(me_s * own + h, 1), :]
        sc = jnp.where(ok, sc, neg_fill)
        top = jnp.max(sc, axis=-1, keepdims=True)
        wt = jnp.where(ok, jnp.exp(sc - top), 0.0)
        weights.append(wt)
        f_max = jnp.where(wide == h, top, f_max)
        f_sum = jnp.where(wide == h, jnp.sum(wt, axis=-1, keepdims=True), f_sum)
    av = jnp.dot(jnp.concatenate(weights, axis=0).astype(bf16), vown[...], preferred_element_type=f32)
    f_acc = jnp.zeros((rows, own_width), f32)
    for h in range(own):
        f_acc = jnp.where(own_lane == h, av[h * rows : (h + 1) * rows], f_acc)

    row_req = iota((rows, 128), 0) >> 3
    spread = (iota((128, own_width), 1) >> 6 == iota((128, own_width), 0)).astype(bf16)
    piece_of = []
    for s in range(n_seq):
        vec = jnp.zeros((rows, 128), jnp.int32)
        for r in range(reqs):
            held = jnp.int32(0)
            for p in range(n_seq):
                held = held + jnp.where(pmap[r * n_seq + p] == s, p, 0)
            vec = jnp.where(row_req == r, held, vec)
        piece_of.append(vec)
    drafted = jnp.zeros((rows, 1), jnp.int32)
    row1 = iota((rows, 1), 0)
    for r in range(reqs):
        drafted = jnp.where(row1 >> 3 == r, drafts[r], drafted)

    for j in range(1, n_seq):
        src = (me_s + j) % n_seq
        pltpu.make_async_remote_copy(
            ssend.at[src], srecv.at[src], s5.at[src], r5.at[src], device_id={"seq": src}, device_id_type=MESH
        ).wait_recv()
    stat = [srecv[s] for s in range(n_seq)]
    sums = [pltpu.roll(a, 96, 1) for a in stat]
    tots = [pltpu.roll(a, 64, 1) for a in stat]
    tops = []
    for a in range(n_seq):
        later = jnp.zeros((rows, 128), f32)
        for b in range(n_seq):
            if a != b:
                later = later + jnp.where(piece_of[b] > piece_of[a], tots[b], 0.0)
        tops.append(stat[a] + later)
    joint = functools.reduce(jnp.maximum, tops, f_max)
    scale = [jnp.exp(t - joint) for t in tops] + [jnp.exp(f_max - joint)]
    whole = functools.reduce(jnp.add, [a * b for a, b in zip(scale, sums + [f_sum])])
    coef = jnp.concatenate([jnp.where(wide < own, a / whole, 0.0) for a in scale], axis=0)
    coef = dot_exact(coef, spread)
    for j in range(1, n_seq):
        src = (me_s + j) % n_seq
        pltpu.make_async_remote_copy(
            asend.at[src], arecv.at[src], s6.at[src], r6.at[src], device_id={"seq": src}, device_id_type=MESH
        ).wait_recv()
    result = coef[n_seq * rows :] * f_acc
    for s in range(n_seq):
        result = result + coef[s * rows : (s + 1) * rows] * arecv[s].astype(f32)
    result = jnp.where(row1 & 7 <= drafted, result, 0.0)
    for m in range(new):
        out[m] = jnp.concatenate(
            [result[r * ROWS + m : r * ROWS + m + 1] for r in range(reqs)], axis=0
        ).astype(bf16)
    for c in sends:
        c.wait_send()


def body(
    hidden_in, norm_gain, w_qkv, w_forget, forget_bias, cache_keys, cache_values, cache_forget,
    cache_lengths, piece_map, draft_counts,
):
    reqs, new, width = hidden_in.shape
    heads = w_forget.shape[1]
    n_half = lax.axis_size("fsdp") // 2
    n_seq = lax.axis_size("seq")
    own, dims = w_qkv.shape[2], w_qkv.shape[3]
    own_width = own * HEAD_DIM
    piece_len = cache_keys.shape[1]
    used = own * dims
    rp = -(-used // 16) * 16
    rows = reqs * ROWS
    part = width // SPLIT

    wt = jnp.transpose(w_qkv, (1, 2, 3, 0)).reshape(3, used, width)
    if rp != used:
        wt = jnp.pad(wt, ((0, 0), (0, rp - used), (0, 0)))
    perm = np.zeros((n_half, 128, own_width), np.float32)
    for z in range(n_half):
        for c in range(2):
            for h in range(own):
                for d in range(dims):
                    perm[z, c * rp + h * dims + d, h * HEAD_DIM + (2 * z + c) * dims + d] = 1.0
    perm = jnp.asarray(perm.reshape(n_half * 128, own_width), bf16)

    cfg = (n_half, n_seq, reqs, new, own, rp)
    vmem = pl.BlockSpec(memory_space=pltpu.VMEM)
    smem = pl.BlockSpec(memory_space=pltpu.SMEM)
    hbm = pl.BlockSpec(memory_space=pl.ANY)
    dma = lambda n: pltpu.SemaphoreType.DMA((n,))
    out = pl.pallas_call(
        functools.partial(kernel, cfg),
        out_shape=jax.ShapeDtypeStruct((new, reqs, own_width), bf16),
        in_specs=[smem] * 3 + [vmem] * 4 + [hbm] * 5,
        out_specs=vmem,
        scratch_shapes=[
            pltpu.VMEM((384, width), bf16),
            pltpu.VMEM((n_half, SPLIT, rows, part), bf16),
            pltpu.VMEM((rows, width), f32),
            pltpu.VMEM((n_half, 3, rows, 128), bf16),
            pltpu.VMEM((n_half, 3, rows, 128), bf16),
            pltpu.VMEM((n_seq, rows, own_width), bf16),
            pltpu.VMEM((rows, width), f32),
            pltpu.VMEM((rows, own_width), bf16),
            pltpu.VMEM((rows, own_width), bf16),
            pltpu.VMEM((reqs, piece_len, width), bf16),
            pltpu.VMEM((reqs, piece_len, width), bf16),
            pltpu.VMEM((n_half * 128, own_width), bf16),
            pltpu.VMEM((reqs, heads, piece_len), f32),
            pltpu.VMEM((reqs, heads, piece_len), f32),
            pltpu.VMEM((heads, rows), f32),
            pltpu.VMEM((rows, width), f32),
            pltpu.VMEM((n_seq, rows, own_width), bf16),
            pltpu.VMEM((n_seq, rows, own_width), bf16),
            pltpu.VMEM((n_seq, rows, 128), f32),
            pltpu.VMEM((n_seq, rows, 128), f32),
            dma(5 + 2 * reqs), dma(3), dma(3), dma(n_half), dma(n_half),
            dma(n_half * SPLIT), dma(n_half * SPLIT), dma(n_half), dma(n_half),
            dma(n_seq), dma(n_seq), dma(n_seq), dma(n_seq), dma(n_seq), dma(n_seq),
        ],
        compiler_params=pltpu.CompilerParams(
            collective_id=0, has_side_effects=True, vmem_limit_bytes=40 * 2**20
        ),
        name="verify_drafts",
    )(
        cache_lengths, piece_map.reshape(-1), draft_counts,
        jnp.transpose(hidden_in, (1, 0, 2)), norm_gain[None, :], w_forget.T, forget_bias[:, None],
        wt, perm, cache_keys, cache_values, cache_forget,
    )
    return jnp.transpose(out, (1, 0, 2))


def solution(mesh):
    in_specs = (
        P("fsdp", None, None),
        P(),
        P(None, None, "seq", "fsdp"),
        P(),
        P(),
        P("fsdp", "seq", None),
        P("fsdp", "seq", None),
        P("fsdp", None, "seq"),
        P("fsdp"),
        P("fsdp", None),
        P("fsdp"),
    )
    out_specs = P("fsdp", None, "seq")
    return jax.shard_map(body, mesh=mesh, in_specs=in_specs, out_specs=out_specs, check_vma=False)
```

```python
import functools

import jax
import jax.numpy as jnp
import numpy as np
from jax import lax
from jax.experimental import pallas as pl
from jax.experimental.pallas import tpu as pltpu
from jax.sharding import PartitionSpec as P

HEAD_DIM = 64
ROWS = 8
SPLIT = 4
TILE = 256
norm_eps = 1e-06
neg_fill = -1e30
f32 = jnp.float32
bf16 = jnp.bfloat16
NT = (((1,), (1,)), ((), ()))


def dot_nt(a, b):
    return lax.dot_general(a, b, NT, preferred_element_type=f32)


def dot_exact(a, ones):
    hi = a.astype(bf16)
    rest = a - hi.astype(f32)
    mid = rest.astype(bf16)
    low = (rest - mid.astype(f32)).astype(bf16)
    n = a.shape[0]
    if n % 16 == 0:
        out = jnp.dot(jnp.concatenate([hi, mid, low], axis=0), ones, preferred_element_type=f32)
        return out[:n] + out[n : 2 * n] + out[2 * n :]
    return sum(jnp.dot(x, ones, preferred_element_type=f32) for x in (hi, mid, low))


def iota(shape, dim):
    return lax.broadcasted_iota(jnp.int32, shape, dim)


def kernel(
    cfg,
    lens, pmap, drafts, bias, hidden, gain, wf, w, perm, kc, vc, fg,
    out,
    wbuf, xs, nf, ysend, yrecv, qall, qf, kown, vown, kv_k, kv_v, permv, fgv, suf, pre, acc,
    asend, arecv, ssend, srecv,
    lsem, wsend, wrecv, s1, r1, s2, r2, s3, r3, s4, r4, s5, r5, s6, r6,
):
    n_half, n_seq, reqs, new, own, rp = cfg
    head_count = wf.shape[0]
    width = hidden.shape[2]
    part = width // SPLIT
    own_width = own * HEAD_DIM
    piece_len = kc.shape[1]
    rows = reqs * ROWS
    me_f = lax.axis_index("fsdp")
    me_s = lax.axis_index("seq")
    me_z = me_f // 2
    me_c = me_f % 2
    sib = me_z * 2 + 1 - me_c
    me_q = me_s % SPLIT
    block = me_s - me_q

    local = [
        pltpu.make_async_copy(fg, fgv, lsem.at[0]),
        pltpu.make_async_copy(perm, permv, lsem.at[1]),
    ]
    wrow = [pl.ds(pl.multiple_of(p * 128 + me_c * rp, 16), rp) for p in range(3)]
    wlocal = [pltpu.make_async_copy(w.at[p], wbuf.at[wrow[p]], lsem.at[2 + p]) for p in range(3)]
    big = []
    for r in range(reqs):
        big.append(pltpu.make_async_copy(kc.at[r], kv_k.at[r], lsem.at[5 + r]))
    for r in range(reqs):
        big.append(pltpu.make_async_copy(vc.at[r], kv_v.at[r], lsem.at[5 + reqs + r]))

    barrier = pltpu.get_barrier_semaphore()
    MESH = pl.DeviceIdType.MESH
    for j in range(1, n_half):
        pl.semaphore_signal(barrier, 1, device_id={"fsdp": (me_z + j) % n_half * 2 + me_c}, device_id_type=MESH)
    for j in range(1, n_seq):
        pl.semaphore_signal(barrier, 1, device_id={"seq": (me_s + j) % n_seq}, device_id_type=MESH)
    pl.semaphore_signal(barrier, 1, device_id={"fsdp": sib}, device_id_type=MESH)
    for c in wlocal + local + big:
        c.start()

    nf[...] = jnp.zeros_like(nf)
    gains = gain[...].reshape(1, width)
    for m in range(new):
        x = hidden[m].astype(f32)
        mean_sq = jnp.mean(x * x, axis=-1, keepdims=True)
        x = x * lax.rsqrt(mean_sq + norm_eps) * gains
        for r in range(reqs):
            nf[r * ROWS + m : r * ROWS + m + 1, :] = x[r : r + 1]
    normed = nf[...].astype(bf16)
    for q in range(SPLIT):
        xs[me_z, q] = normed[:, q * part : (q + 1) * part]
    if 2 * rp < 128:
        for p in range(3):
            wbuf[p * 128 + 2 * rp : (p + 1) * 128, :] = jnp.zeros((128 - 2 * rp, width), bf16)

    pl.semaphore_wait(barrier, n_half + n_seq - 1)

    sends = []
    first = []
    for j in range(1, n_half):
        peer = (me_z + j) % n_half
        c = pltpu.make_async_remote_copy(
            xs.at[me_z, me_q], xs.at[me_z, me_q], s1.at[peer], r1.at[me_z],
            device_id={"fsdp": peer * 2 + me_c}, device_id_type=MESH,
        )
        c.start()
        sends.append(c)
    for p in range(3):
        c = pltpu.make_async_remote_copy(
            w.at[p], wbuf.at[wrow[p]], wsend.at[p], wrecv.at[p],
            device_id={"fsdp": sib}, device_id_type=MESH,
        )
        c.start()
        sends.append(c)

    local[0].wait()
    lane = iota((1, piece_len), 1)

    def limit_of(r):
        slot = jnp.int32(0)
        for p in range(n_seq):
            slot = slot + jnp.where(pmap[r, p] == me_s, p, 0)
        return lens[r] - slot * piece_len

    for r in range(reqs):
        fgv[r] = jnp.where(lane < limit_of(r), fgv[r], 0.0)
    after = (iota((piece_len, piece_len), 0) > iota((piece_len, piece_len), 1)).astype(bf16)
    masked = jnp.concatenate([fgv[r] for r in range(reqs)], axis=0)
    trailing = dot_exact(masked, after)
    for r in range(reqs):
        suf[r] = trailing[r * head_count : (r + 1) * head_count]

    head_row = iota((head_count, rows), 0)
    shift = jnp.zeros((head_count, rows), f32)
    for h in range(head_count):
        shift = jnp.where(head_row == h, bias[h], shift)
    gate = dot_nt(wf[...], normed) + shift
    gate = jnp.minimum(gate, 0.0) - jnp.log(1.0 + jnp.exp(-jnp.abs(gate)))
    ir, ic = iota((rows, rows), 0), iota((rows, rows), 1)
    upto = ((ir >> 3 == ic >> 3) & (ir <= ic)).astype(bf16)
    pre[...] = dot_exact(gate, upto)

    for j in range(n_half):
        src = (me_z + j) % n_half
        if j:
            pltpu.make_async_remote_copy(
                xs.at[src, me_q], xs.at[src, me_q], s1.at[src], r1.at[src],
                device_id={"fsdp": src * 2 + me_c}, device_id_type=MESH,
            ).wait_recv()
            for i in range(1, SPLIT):
                to = (me_q + i) % SPLIT
                c = pltpu.make_async_remote_copy(
                    xs.at[src, me_q], xs.at[src, me_q], s2.at[src * SPLIT + to], r2.at[src * SPLIT + me_q],
                    device_id={"seq": block + to}, device_id_type=MESH,
                )
                c.start()
                sends.append(c)
    for c in wlocal:
        c.wait()
    for c in sends[n_half - 1 : n_half + 2]:
        c.wait_recv()
    for j in range(1, n_half):
        src = (me_z + j) % n_half
        for i in range(1, SPLIT):
            q = (me_q + i) % SPLIT
            pltpu.make_async_remote_copy(
                xs.at[src, q], xs.at[src, q], s2.at[src * SPLIT + q], r2.at[src * SPLIT + q],
                device_id={"seq": block + q}, device_id_type=MESH,
            ).wait_recv()

    total = jnp.zeros((n_half * rows, 384), f32)
    for q in range(SPLIT):
        x = jnp.concatenate([xs[z, q] for z in range(n_half)], axis=0)
        total = total + dot_nt(x, wbuf[:, q * part : (q + 1) * part])
    proj = total.astype(bf16)
    for z in range(n_half):
        for p in range(3):
            ysend[z, p] = proj[z * rows : (z + 1) * rows, p * 128 : (p + 1) * 128]
    for j in range(1, n_half):
        peer = (me_z + j) % n_half
        c = pltpu.make_async_remote_copy(
            ysend.at[peer], yrecv.at[me_z], s3.at[peer], r3.at[me_z],
            device_id={"fsdp": peer * 2 + me_c}, device_id_type=MESH,
        )
        c.start()
        sends.append(c)
    yrecv[me_z] = ysend[me_z]
    local[1].wait()
    for j in range(1, n_half):
        src = (me_z + j) % n_half
        pltpu.make_async_remote_copy(
            ysend.at[src], yrecv.at[src], s3.at[src], r3.at[src],
            device_id={"fsdp": src * 2 + me_c}, device_id_type=MESH,
        ).wait_recv()
    y = jnp.concatenate(
        [jnp.concatenate([yrecv[z, p] for z in range(n_half)], axis=1) for p in range(3)], axis=0
    )
    qkv = jnp.dot(y, permv[...], preferred_element_type=f32).astype(bf16)
    qall[me_s] = qkv[:rows]
    kown[...] = qkv[rows : 2 * rows]
    vown[...] = qkv[2 * rows :]
    for j in range(1, n_seq):
        peer = (me_s + j) % n_seq
        c = pltpu.make_async_remote_copy(
            qall.at[me_s], qall.at[me_s], s4.at[peer], r4.at[me_s],
            device_id={"seq": peer}, device_id_type=MESH,
        )
        c.start()
        sends.append(c)
    for j in range(1, n_seq):
        src = (me_s + j) % n_seq
        pltpu.make_async_remote_copy(
            qall.at[src], qall.at[src], s4.at[src], r4.at[src],
            device_id={"seq": src}, device_id_type=MESH,
        ).wait_recv()
    qf[...] = jnp.concatenate([qall[s].astype(f32) for s in range(n_seq)], axis=1) * (HEAD_DIM**-0.5)

    for c in big:
        c.wait()

    lane_head = iota((ROWS, TILE), 1) >> 6
    stat_lane = iota((ROWS, 128), 1)
    per = TILE // HEAD_DIM

    def request(r, carry):
        at = pl.ds(pl.multiple_of(r * ROWS, ROWS), ROWS)
        live = lane < limit_of(r)
        stats = [jnp.zeros((ROWS, 128), f32) for _ in range(n_seq)]
        for g in range(width // TILE):
            cols = slice(g * TILE, (g + 1) * TILE)
            heads = slice(g * per, (g + 1) * per)
            q = qf[at, cols]
            qb = jnp.concatenate([jnp.where(lane_head == h, q, 0.0) for h in range(per)], axis=0).astype(bf16)
            sc = dot_nt(qb, kv_k[r, :, cols])
            trail = suf[r, heads, :]
            sc = sc + jnp.broadcast_to(trail[:, None, :], (per, ROWS, piece_len)).reshape(per * ROWS, piece_len)
            sc = jnp.where(live, sc, neg_fill)
            top = jnp.max(sc, axis=-1, keepdims=True)
            wt = jnp.where(live, jnp.exp(sc - top), 0.0)
            sums = jnp.sum(wt, axis=-1, keepdims=True)
            av = jnp.dot(wt.astype(bf16), kv_v[r, :, cols], preferred_element_type=f32)
            got = jnp.zeros((ROWS, TILE), f32)
            piece_sum = jnp.sum(fgv[r, heads, :], axis=-1, keepdims=True)
            for h in range(per):
                hr = slice(h * ROWS, (h + 1) * ROWS)
                got = jnp.where(lane_head == h, av[hr], got)
                s, hl = divmod(g * per + h, own)
                t = jnp.where(stat_lane == hl, top[hr], stats[s])
                t = jnp.where(stat_lane == 32 + hl, sums[hr], t)
                stats[s] = jnp.where(stat_lane == 64 + hl, piece_sum[h : h + 1], t)
            acc[at, cols] = got
        for s in range(n_seq):
            ssend[s, at, :] = stats[s]
        return carry

    lax.fori_loop(0, reqs, request, 0)
    for s in range(n_seq):
        asend[s] = acc[:, s * own_width : (s + 1) * own_width].astype(bf16)
    for j in range(1, n_seq):
        peer = (me_s + j) % n_seq
        for c in (
            pltpu.make_async_remote_copy(
                ssend.at[peer], srecv.at[me_s], s5.at[peer], r5.at[me_s],
                device_id={"seq": peer}, device_id_type=MESH,
            ),
            pltpu.make_async_remote_copy(
                asend.at[peer], arecv.at[me_s], s6.at[peer], r6.at[me_s],
                device_id={"seq": peer}, device_id_type=MESH,
            ),
        ):
            c.start()
            sends.append(c)
    arecv[me_s] = asend[me_s]
    srecv[me_s] = ssend[me_s]

    own_lane = iota((rows, own_width), 1) >> 6
    qo = qall[me_s].astype(f32) * (HEAD_DIM**-0.5)
    qb = jnp.concatenate([jnp.where(own_lane == h, qo, 0.0) for h in range(own)], axis=0).astype(bf16)
    fresh = dot_nt(qb, kown[...])
    ok = (ir >> 3 == ic >> 3) & (ic & 7 <= ir & 7) & (ic & 7 < new)
    wide = iota((rows, 128), 1)
    f_max = jnp.zeros((rows, 128), f32)
    f_sum = jnp.zeros((rows, 128), f32)
    weights = []
    for h in range(own):
        sc = fresh[h * rows : (h + 1) * rows] - pre[pl.ds(me_s * own + h, 1), :]
        sc = jnp.where(ok, sc, neg_fill)
        top = jnp.max(sc, axis=-1, keepdims=True)
        wt = jnp.where(ok, jnp.exp(sc - top), 0.0)
        weights.append(wt)
        f_max = jnp.where(wide == h, top, f_max)
        f_sum = jnp.where(wide == h, jnp.sum(wt, axis=-1, keepdims=True), f_sum)
    av = jnp.dot(jnp.concatenate(weights, axis=0).astype(bf16), vown[...], preferred_element_type=f32)
    f_acc = jnp.zeros((rows, own_width), f32)
    for h in range(own):
        f_acc = jnp.where(own_lane == h, av[h * rows : (h + 1) * rows], f_acc)

    row_req = iota((rows, 128), 0) >> 3
    spread = (iota((128, own_width), 1) >> 6 == iota((128, own_width), 0)).astype(bf16)
    piece_of = []
    for s in range(n_seq):
        vec = jnp.zeros((rows, 128), jnp.int32)
        for r in range(reqs):
            held = jnp.int32(0)
            for p in range(n_seq):
                held = held + jnp.where(pmap[r, p] == s, p, 0)
            vec = jnp.where(row_req == r, held, vec)
        piece_of.append(vec)
    drafted = jnp.zeros((rows, 1), jnp.int32)
    row1 = iota((rows, 1), 0)
    for r in range(reqs):
        drafted = jnp.where(row1 >> 3 == r, drafts[r], drafted)

    for j in range(1, n_seq):
        src = (me_s + j) % n_seq
        pltpu.make_async_remote_copy(
            ssend.at[src], srecv.at[src], s5.at[src], r5.at[src], device_id={"seq": src}, device_id_type=MESH
        ).wait_recv()
    stat = [srecv[s] for s in range(n_seq)]
    sums = [pltpu.roll(a, 96, 1) for a in stat]
    tots = [pltpu.roll(a, 64, 1) for a in stat]
    tops = []
    for a in range(n_seq):
        later = jnp.zeros((rows, 128), f32)
        for b in range(n_seq):
            if a != b:
                later = later + jnp.where(piece_of[b] > piece_of[a], tots[b], 0.0)
        tops.append(stat[a] + later)
    joint = functools.reduce(jnp.maximum, tops, f_max)
    scale = [jnp.exp(t - joint) for t in tops] + [jnp.exp(f_max - joint)]
    whole = functools.reduce(jnp.add, [a * b for a, b in zip(scale, sums + [f_sum])])
    coef = jnp.concatenate([jnp.where(wide < own, a / whole, 0.0) for a in scale], axis=0)
    coef = dot_exact(coef, spread)
    for j in range(1, n_seq):
        src = (me_s + j) % n_seq
        pltpu.make_async_remote_copy(
            asend.at[src], arecv.at[src], s6.at[src], r6.at[src], device_id={"seq": src}, device_id_type=MESH
        ).wait_recv()
    result = coef[n_seq * rows :] * f_acc
    for s in range(n_seq):
        result = result + coef[s * rows : (s + 1) * rows] * arecv[s].astype(f32)
    result = jnp.where(row1 & 7 <= drafted, result, 0.0)
    for m in range(new):
        out[m] = jnp.concatenate(
            [result[r * ROWS + m : r * ROWS + m + 1] for r in range(reqs)], axis=0
        ).astype(bf16)
    for c in sends:
        c.wait_send()


def body(
    hidden_in, norm_gain, w_qkv, w_forget, forget_bias, cache_keys, cache_values, cache_forget,
    cache_lengths, piece_map, draft_counts,
):
    reqs, new, width = hidden_in.shape
    heads = w_forget.shape[1]
    n_half = lax.axis_size("fsdp") // 2
    n_seq = lax.axis_size("seq")
    own, dims = w_qkv.shape[2], w_qkv.shape[3]
    own_width = own * HEAD_DIM
    piece_len = cache_keys.shape[1]
    used = own * dims
    rp = -(-used // 16) * 16
    rows = reqs * ROWS
    part = width // SPLIT

    wt = jnp.transpose(w_qkv, (1, 2, 3, 0)).reshape(3, used, width)
    if rp != used:
        wt = jnp.pad(wt, ((0, 0), (0, rp - used), (0, 0)))
    perm = np.zeros((n_half, 128, own_width), np.float32)
    for z in range(n_half):
        for c in range(2):
            for h in range(own):
                for d in range(dims):
                    perm[z, c * rp + h * dims + d, h * HEAD_DIM + (2 * z + c) * dims + d] = 1.0
    perm = jnp.asarray(perm.reshape(n_half * 128, own_width), bf16)

    cfg = (n_half, n_seq, reqs, new, own, rp)
    vmem = pl.BlockSpec(memory_space=pltpu.VMEM)
    smem = pl.BlockSpec(memory_space=pltpu.SMEM)
    hbm = pl.BlockSpec(memory_space=pltpu.HBM)
    dma = lambda n: pltpu.SemaphoreType.DMA((n,))
    out = pl.pallas_call(
        functools.partial(kernel, cfg),
        out_shape=jax.ShapeDtypeStruct((new, reqs, own_width), bf16),
        in_specs=[smem] * 4 + [vmem] * 3 + [hbm] * 5,
        out_specs=vmem,
        scratch_shapes=[
            pltpu.VMEM((384, width), bf16),
            pltpu.VMEM((n_half, SPLIT, rows, part), bf16),
            pltpu.VMEM((rows, width), f32),
            pltpu.VMEM((n_half, 3, rows, 128), bf16),
            pltpu.VMEM((n_half, 3, rows, 128), bf16),
            pltpu.VMEM((n_seq, rows, own_width), bf16),
            pltpu.VMEM((rows, width), f32),
            pltpu.VMEM((rows, own_width), bf16),
            pltpu.VMEM((rows, own_width), bf16),
            pltpu.VMEM((reqs, piece_len, width), bf16),
            pltpu.VMEM((reqs, piece_len, width), bf16),
            pltpu.VMEM((n_half * 128, own_width), bf16),
            pltpu.VMEM((reqs, heads, piece_len), f32),
            pltpu.VMEM((reqs, heads, piece_len), f32),
            pltpu.VMEM((heads, rows), f32),
            pltpu.VMEM((rows, width), f32),
            pltpu.VMEM((n_seq, rows, own_width), bf16),
            pltpu.VMEM((n_seq, rows, own_width), bf16),
            pltpu.VMEM((n_seq, rows, 128), f32),
            pltpu.VMEM((n_seq, rows, 128), f32),
            dma(5 + 2 * reqs), dma(3), dma(3), dma(n_half), dma(n_half),
            dma(n_half * SPLIT), dma(n_half * SPLIT), dma(n_half), dma(n_half),
            dma(n_seq), dma(n_seq), dma(n_seq), dma(n_seq), dma(n_seq), dma(n_seq),
        ],
        compiler_params=pltpu.CompilerParams(
            collective_id=0, has_side_effects=True, vmem_limit_bytes=60 * 2**20
        ),
        name="verify_drafts",
    )(
        cache_lengths, piece_map, draft_counts, forget_bias,
        jnp.transpose(hidden_in, (1, 0, 2)), norm_gain, w_forget.T,
        wt, perm, cache_keys, cache_values, cache_forget,
    )
    return jnp.transpose(out, (1, 0, 2))


def solution(mesh):
    in_specs = (
        P("fsdp", None, None),
        P(),
        P(None, None, "seq", "fsdp"),
        P(),
        P(),
        P("fsdp", "seq", None),
        P("fsdp", "seq", None),
        P("fsdp", None, "seq"),
        P("fsdp"),
        P("fsdp", None),
        P("fsdp"),
    )
    out_specs = P("fsdp", None, "seq")
    return jax.shard_map(body, mesh=mesh, in_specs=in_specs, out_specs=out_specs, check_vma=False)
```

```python
import functools

import jax
import jax.numpy as jnp
import numpy as np
from jax import lax
from jax.experimental import pallas as pl
from jax.experimental.pallas import tpu as pltpu
from jax.sharding import PartitionSpec as P

HEAD_DIM = 64
ROWS = 8
SPLIT = 4
TILE = 256
norm_eps = 1e-06
neg_fill = -1e30
f32 = jnp.float32
bf16 = jnp.bfloat16
NT = (((1,), (1,)), ((), ()))


def dot_nt(a, b):
    return lax.dot_general(a, b, NT, preferred_element_type=f32)


def dot_exact(a, ones):
    hi = a.astype(bf16)
    rest = a - hi.astype(f32)
    mid = rest.astype(bf16)
    low = (rest - mid.astype(f32)).astype(bf16)
    n = a.shape[0]
    if n % 16 == 0:
        out = jnp.dot(jnp.concatenate([hi, mid, low], axis=0), ones, preferred_element_type=f32)
        return out[:n] + out[n : 2 * n] + out[2 * n :]
    return sum(jnp.dot(x, ones, preferred_element_type=f32) for x in (hi, mid, low))


def iota(shape, dim):
    return lax.broadcasted_iota(jnp.int32, shape, dim)


def kernel(
    cfg,
    lens, pmap, drafts, bias, hidden, gain, wf, w, perm, kc, vc, fg,
    out,
    wbuf, xs, nf, ysend, yrecv, qall, qf, kown, vown, kv_k, kv_v, permv, fgv, suf, pre, acc,
    asend, arecv, ssend, srecv,
    lsem, wsend, wrecv, s1, r1, s2, r2, s3, r3, s4, r4, s5, r5, s6, r6,
):
    n_half, n_seq, reqs, new, own, rp = cfg
    head_count = wf.shape[0]
    width = hidden.shape[2]
    part = width // SPLIT
    own_width = own * HEAD_DIM
    piece_len = kc.shape[1]
    rows = reqs * ROWS
    me_f = lax.axis_index("fsdp")
    me_s = lax.axis_index("seq")
    me_z = me_f // 2
    me_c = me_f % 2
    sib = me_z * 2 + 1 - me_c
    me_q = me_s % SPLIT
    block = me_s - me_q

    local = [
        pltpu.make_async_copy(fg, fgv, lsem.at[0]),
        pltpu.make_async_copy(perm, permv, lsem.at[1]),
    ]
    wrow = [pl.ds(pl.multiple_of(p * 128 + me_c * rp, 16), rp) for p in range(3)]
    wlocal = [pltpu.make_async_copy(w.at[p], wbuf.at[wrow[p]], lsem.at[2 + p]) for p in range(3)]
    big = []
    for r in range(reqs):
        big.append(pltpu.make_async_copy(kc.at[r], kv_k.at[r], lsem.at[5 + r]))
    for r in range(reqs):
        big.append(pltpu.make_async_copy(vc.at[r], kv_v.at[r], lsem.at[5 + reqs + r]))

    barrier = pltpu.get_barrier_semaphore()
    MESH = pl.DeviceIdType.MESH
    for j in range(1, n_half):
        pl.semaphore_signal(barrier, 1, device_id={"fsdp": (me_z + j) % n_half * 2 + me_c}, device_id_type=MESH)
    for j in range(1, n_seq):
        pl.semaphore_signal(barrier, 1, device_id={"seq": (me_s + j) % n_seq}, device_id_type=MESH)
    pl.semaphore_signal(barrier, 1, device_id={"fsdp": sib}, device_id_type=MESH)
    for c in wlocal + local + big:
        c.start()

    nf[...] = jnp.zeros_like(nf)
    gains = gain[...].reshape(1, width)
    for m in range(new):
        x = hidden[m].astype(f32)
        mean_sq = jnp.mean(x * x, axis=-1, keepdims=True)
        x = x * lax.rsqrt(mean_sq + norm_eps) * gains
        for r in range(reqs):
            nf[r * ROWS + m : r * ROWS + m + 1, :] = x[r : r + 1]
    normed = nf[...].astype(bf16)
    for q in range(SPLIT):
        xs[me_z, q] = normed[:, q * part : (q + 1) * part]
    if 2 * rp < 128:
        for p in range(3):
            wbuf[p * 128 + 2 * rp : (p + 1) * 128, :] = jnp.zeros((128 - 2 * rp, width), bf16)

    pl.semaphore_wait(barrier, n_half + n_seq - 1)

    sends = []
    first = []
    for j in range(1, n_half):
        peer = (me_z + j) % n_half
        c = pltpu.make_async_remote_copy(
            xs.at[me_z, me_q], xs.at[me_z, me_q], s1.at[peer], r1.at[me_z],
            device_id={"fsdp": peer * 2 + me_c}, device_id_type=MESH,
        )
        c.start()
        sends.append(c)
    for p in range(3):
        c = pltpu.make_async_remote_copy(
            w.at[p], wbuf.at[wrow[p]], wsend.at[p], wrecv.at[p],
            device_id={"fsdp": sib}, device_id_type=MESH,
        )
        c.start()
        sends.append(c)

    lane = iota((1, piece_len), 1)

    def limit_of(r):
        slot = jnp.int32(0)
        for p in range(n_seq):
            slot = slot + jnp.where(pmap[r, p] == me_s, p, 0)
        return lens[r] - slot * piece_len

    for j in range(n_half):
        src = (me_z + j) % n_half
        if j:
            pltpu.make_async_remote_copy(
                xs.at[src, me_q], xs.at[src, me_q], s1.at[src], r1.at[src],
                device_id={"fsdp": src * 2 + me_c}, device_id_type=MESH,
            ).wait_recv()
            for i in range(1, SPLIT):
                to = (me_q + i) % SPLIT
                c = pltpu.make_async_remote_copy(
                    xs.at[src, me_q], xs.at[src, me_q], s2.at[src * SPLIT + to], r2.at[src * SPLIT + me_q],
                    device_id={"seq": block + to}, device_id_type=MESH,
                )
                c.start()
                sends.append(c)
    local[0].wait()
    for r in range(reqs):
        fgv[r] = jnp.where(lane < limit_of(r), fgv[r], 0.0)
    after = (iota((piece_len, piece_len), 0) > iota((piece_len, piece_len), 1)).astype(bf16)
    masked = jnp.concatenate([fgv[r] for r in range(reqs)], axis=0)
    trailing = dot_exact(masked, after)
    for r in range(reqs):
        suf[r] = trailing[r * head_count : (r + 1) * head_count]

    for c in wlocal:
        c.wait()
    for c in sends[n_half - 1 : n_half + 2]:
        c.wait_recv()
    for j in range(1, n_half):
        src = (me_z + j) % n_half
        for i in range(1, SPLIT):
            q = (me_q + i) % SPLIT
            pltpu.make_async_remote_copy(
                xs.at[src, q], xs.at[src, q], s2.at[src * SPLIT + q], r2.at[src * SPLIT + q],
                device_id={"seq": block + q}, device_id_type=MESH,
            ).wait_recv()

    total = jnp.zeros((n_half * rows, 384), f32)
    for q in range(SPLIT):
        x = jnp.concatenate([xs[z, q] for z in range(n_half)], axis=0)
        total = total + dot_nt(x, wbuf[:, q * part : (q + 1) * part])
    proj = total.astype(bf16)
    for z in range(n_half):
        for p in range(3):
            ysend[z, p] = proj[z * rows : (z + 1) * rows, p * 128 : (p + 1) * 128]
    for j in range(1, n_half):
        peer = (me_z + j) % n_half
        c = pltpu.make_async_remote_copy(
            ysend.at[peer], yrecv.at[me_z], s3.at[peer], r3.at[me_z],
            device_id={"fsdp": peer * 2 + me_c}, device_id_type=MESH,
        )
        c.start()
        sends.append(c)
    yrecv[me_z] = ysend[me_z]
    local[1].wait()
    head_row = iota((head_count, rows), 0)
    shift = jnp.zeros((head_count, rows), f32)
    for h in range(head_count):
        shift = jnp.where(head_row == h, bias[h], shift)
    gate = dot_nt(wf[...], normed) + shift
    gate = jnp.minimum(gate, 0.0) - jnp.log(1.0 + jnp.exp(-jnp.abs(gate)))
    ir, ic = iota((rows, rows), 0), iota((rows, rows), 1)
    upto = ((ir >> 3 == ic >> 3) & (ir <= ic)).astype(bf16)
    pre[...] = dot_exact(gate, upto)

    for j in range(1, n_half):
        src = (me_z + j) % n_half
        pltpu.make_async_remote_copy(
            ysend.at[src], yrecv.at[src], s3.at[src], r3.at[src],
            device_id={"fsdp": src * 2 + me_c}, device_id_type=MESH,
        ).wait_recv()
    y = jnp.concatenate(
        [jnp.concatenate([yrecv[z, p] for z in range(n_half)], axis=1) for p in range(3)], axis=0
    )
    qkv = jnp.dot(y, permv[...], preferred_element_type=f32).astype(bf16)
    qall[me_s] = qkv[:rows]
    kown[...] = qkv[rows : 2 * rows]
    vown[...] = qkv[2 * rows :]
    for j in range(1, n_seq):
        peer = (me_s + j) % n_seq
        c = pltpu.make_async_remote_copy(
            qall.at[me_s], qall.at[me_s], s4.at[peer], r4.at[me_s],
            device_id={"seq": peer}, device_id_type=MESH,
        )
        c.start()
        sends.append(c)
    own_lane = iota((rows, own_width), 1) >> 6
    qo = qall[me_s].astype(f32) * (HEAD_DIM**-0.5)
    qb = jnp.concatenate([jnp.where(own_lane == h, qo, 0.0) for h in range(own)], axis=0).astype(bf16)
    fresh = dot_nt(qb, kown[...])
    ok = (ir >> 3 == ic >> 3) & (ic & 7 <= ir & 7) & (ic & 7 < new)
    wide = iota((rows, 128), 1)
    f_max = jnp.zeros((rows, 128), f32)
    f_sum = jnp.zeros((rows, 128), f32)
    weights = []
    for h in range(own):
        sc = fresh[h * rows : (h + 1) * rows] - pre[pl.ds(me_s * own + h, 1), :]
        sc = jnp.where(ok, sc, neg_fill)
        top = jnp.max(sc, axis=-1, keepdims=True)
        wt = jnp.where(ok, jnp.exp(sc - top), 0.0)
        weights.append(wt)
        f_max = jnp.where(wide == h, top, f_max)
        f_sum = jnp.where(wide == h, jnp.sum(wt, axis=-1, keepdims=True), f_sum)
    av = jnp.dot(jnp.concatenate(weights, axis=0).astype(bf16), vown[...], preferred_element_type=f32)
    f_acc = jnp.zeros((rows, own_width), f32)
    for h in range(own):
        f_acc = jnp.where(own_lane == h, av[h * rows : (h + 1) * rows], f_acc)

    for j in range(1, n_seq):
        src = (me_s + j) % n_seq
        pltpu.make_async_remote_copy(
            qall.at[src], qall.at[src], s4.at[src], r4.at[src],
            device_id={"seq": src}, device_id_type=MESH,
        ).wait_recv()
    qf[...] = jnp.concatenate([qall[s].astype(f32) for s in range(n_seq)], axis=1) * (HEAD_DIM**-0.5)

    for c in big:
        c.wait()

    lane_head = iota((ROWS, TILE), 1) >> 6
    stat_lane = iota((ROWS, 128), 1)
    per = TILE // HEAD_DIM

    def request(r, carry):
        at = pl.ds(pl.multiple_of(r * ROWS, ROWS), ROWS)
        live = lane < limit_of(r)
        stats = [jnp.zeros((ROWS, 128), f32) for _ in range(n_seq)]
        for g in range(width // TILE):
            cols = slice(g * TILE, (g + 1) * TILE)
            heads = slice(g * per, (g + 1) * per)
            q = qf[at, cols]
            qb = jnp.concatenate([jnp.where(lane_head == h, q, 0.0) for h in range(per)], axis=0).astype(bf16)
            sc = dot_nt(qb, kv_k[r, :, cols])
            trail = suf[r, heads, :]
            sc = sc + jnp.broadcast_to(trail[:, None, :], (per, ROWS, piece_len)).reshape(per * ROWS, piece_len)
            sc = jnp.where(live, sc, neg_fill)
            top = jnp.max(sc, axis=-1, keepdims=True)
            wt = jnp.where(live, jnp.exp(sc - top), 0.0)
            sums = jnp.sum(wt, axis=-1, keepdims=True)
            av = jnp.dot(wt.astype(bf16), kv_v[r, :, cols], preferred_element_type=f32)
            got = jnp.zeros((ROWS, TILE), f32)
            piece_sum = jnp.sum(fgv[r, heads, :], axis=-1, keepdims=True)
            for h in range(per):
                hr = slice(h * ROWS, (h + 1) * ROWS)
                got = jnp.where(lane_head == h, av[hr], got)
                s, hl = divmod(g * per + h, own)
                t = jnp.where(stat_lane == hl, top[hr], stats[s])
                t = jnp.where(stat_lane == 32 + hl, sums[hr], t)
                stats[s] = jnp.where(stat_lane == 64 + hl, piece_sum[h : h + 1], t)
            acc[at, cols] = got
        for s in range(n_seq):
            ssend[s, at, :] = stats[s]
        return carry

    lax.fori_loop(0, reqs, request, 0, unroll=True)
    for s in range(n_seq):
        asend[s] = acc[:, s * own_width : (s + 1) * own_width].astype(bf16)
    for j in range(1, n_seq):
        peer = (me_s + j) % n_seq
        for c in (
            pltpu.make_async_remote_copy(
                ssend.at[peer], srecv.at[me_s], s5.at[peer], r5.at[me_s],
                device_id={"seq": peer}, device_id_type=MESH,
            ),
            pltpu.make_async_remote_copy(
                asend.at[peer], arecv.at[me_s], s6.at[peer], r6.at[me_s],
                device_id={"seq": peer}, device_id_type=MESH,
            ),
        ):
            c.start()
            sends.append(c)
    arecv[me_s] = asend[me_s]
    srecv[me_s] = ssend[me_s]

    row_req = iota((rows, 128), 0) >> 3
    spread = (iota((128, own_width), 1) >> 6 == iota((128, own_width), 0)).astype(bf16)
    piece_of = []
    for s in range(n_seq):
        vec = jnp.zeros((rows, 128), jnp.int32)
        for r in range(reqs):
            held = jnp.int32(0)
            for p in range(n_seq):
                held = held + jnp.where(pmap[r, p] == s, p, 0)
            vec = jnp.where(row_req == r, held, vec)
        piece_of.append(vec)
    drafted = jnp.zeros((rows, 1), jnp.int32)
    row1 = iota((rows, 1), 0)
    for r in range(reqs):
        drafted = jnp.where(row1 >> 3 == r, drafts[r], drafted)

    for j in range(1, n_seq):
        src = (me_s + j) % n_seq
        pltpu.make_async_remote_copy(
            ssend.at[src], srecv.at[src], s5.at[src], r5.at[src], device_id={"seq": src}, device_id_type=MESH
        ).wait_recv()
    stat = [srecv[s] for s in range(n_seq)]
    sums = [pltpu.roll(a, 96, 1) for a in stat]
    tots = [pltpu.roll(a, 64, 1) for a in stat]
    tops = []
    for a in range(n_seq):
        later = jnp.zeros((rows, 128), f32)
        for b in range(n_seq):
            if a != b:
                later = later + jnp.where(piece_of[b] > piece_of[a], tots[b], 0.0)
        tops.append(stat[a] + later)
    joint = functools.reduce(jnp.maximum, tops, f_max)
    scale = [jnp.exp(t - joint) for t in tops] + [jnp.exp(f_max - joint)]
    whole = functools.reduce(jnp.add, [a * b for a, b in zip(scale, sums + [f_sum])])
    coef = jnp.concatenate([jnp.where(wide < own, a / whole, 0.0) for a in scale], axis=0)
    coef = dot_exact(coef, spread)
    for j in range(1, n_seq):
        src = (me_s + j) % n_seq
        pltpu.make_async_remote_copy(
            asend.at[src], arecv.at[src], s6.at[src], r6.at[src], device_id={"seq": src}, device_id_type=MESH
        ).wait_recv()
    result = coef[n_seq * rows :] * f_acc
    for s in range(n_seq):
        result = result + coef[s * rows : (s + 1) * rows] * arecv[s].astype(f32)
    result = jnp.where(row1 & 7 <= drafted, result, 0.0)
    for m in range(new):
        out[m] = jnp.concatenate(
            [result[r * ROWS + m : r * ROWS + m + 1] for r in range(reqs)], axis=0
        ).astype(bf16)
    for c in sends:
        c.wait_send()


def body(
    hidden_in, norm_gain, w_qkv, w_forget, forget_bias, cache_keys, cache_values, cache_forget,
    cache_lengths, piece_map, draft_counts,
):
    reqs, new, width = hidden_in.shape
    heads = w_forget.shape[1]
    n_half = lax.axis_size("fsdp") // 2
    n_seq = lax.axis_size("seq")
    own, dims = w_qkv.shape[2], w_qkv.shape[3]
    own_width = own * HEAD_DIM
    piece_len = cache_keys.shape[1]
    used = own * dims
    rp = -(-used // 16) * 16
    rows = reqs * ROWS
    part = width // SPLIT

    wt = jnp.transpose(w_qkv, (1, 2, 3, 0)).reshape(3, used, width)
    if rp != used:
        wt = jnp.pad(wt, ((0, 0), (0, rp - used), (0, 0)))
    perm = np.zeros((n_half, 128, own_width), np.float32)
    for z in range(n_half):
        for c in range(2):
            for h in range(own):
                for d in range(dims):
                    perm[z, c * rp + h * dims + d, h * HEAD_DIM + (2 * z + c) * dims + d] = 1.0
    perm = jnp.asarray(perm.reshape(n_half * 128, own_width), bf16)

    cfg = (n_half, n_seq, reqs, new, own, rp)
    vmem = pl.BlockSpec(memory_space=pltpu.VMEM)
    smem = pl.BlockSpec(memory_space=pltpu.SMEM)
    hbm = pl.BlockSpec(memory_space=pltpu.HBM)
    dma = lambda n: pltpu.SemaphoreType.DMA((n,))
    out = pl.pallas_call(
        functools.partial(kernel, cfg),
        out_shape=jax.ShapeDtypeStruct((new, reqs, own_width), bf16),
        in_specs=[smem] * 4 + [vmem] * 3 + [hbm] * 5,
        out_specs=vmem,
        scratch_shapes=[
            pltpu.VMEM((384, width), bf16),
            pltpu.VMEM((n_half, SPLIT, rows, part), bf16),
            pltpu.VMEM((rows, width), f32),
            pltpu.VMEM((n_half, 3, rows, 128), bf16),
            pltpu.VMEM((n_half, 3, rows, 128), bf16),
            pltpu.VMEM((n_seq, rows, own_width), bf16),
            pltpu.VMEM((rows, width), f32),
            pltpu.VMEM((rows, own_width), bf16),
            pltpu.VMEM((rows, own_width), bf16),
            pltpu.VMEM((reqs, piece_len, width), bf16),
            pltpu.VMEM((reqs, piece_len, width), bf16),
            pltpu.VMEM((n_half * 128, own_width), bf16),
            pltpu.VMEM((reqs, heads, piece_len), f32),
            pltpu.VMEM((reqs, heads, piece_len), f32),
            pltpu.VMEM((heads, rows), f32),
            pltpu.VMEM((rows, width), f32),
            pltpu.VMEM((n_seq, rows, own_width), bf16),
            pltpu.VMEM((n_seq, rows, own_width), bf16),
            pltpu.VMEM((n_seq, rows, 128), f32),
            pltpu.VMEM((n_seq, rows, 128), f32),
            dma(5 + 2 * reqs), dma(3), dma(3), dma(n_half), dma(n_half),
            dma(n_half * SPLIT), dma(n_half * SPLIT), dma(n_half), dma(n_half),
            dma(n_seq), dma(n_seq), dma(n_seq), dma(n_seq), dma(n_seq), dma(n_seq),
        ],
        compiler_params=pltpu.CompilerParams(
            collective_id=0, has_side_effects=True, vmem_limit_bytes=60 * 2**20
        ),
        name="verify_drafts",
    )(
        cache_lengths, piece_map, draft_counts, forget_bias,
        jnp.transpose(hidden_in, (1, 0, 2)), norm_gain, w_forget.T,
        wt, perm, cache_keys, cache_values, cache_forget,
    )
    return jnp.transpose(out, (1, 0, 2))


def solution(mesh):
    in_specs = (
        P("fsdp", None, None),
        P(),
        P(None, None, "seq", "fsdp"),
        P(),
        P(),
        P("fsdp", "seq", None),
        P("fsdp", "seq", None),
        P("fsdp", None, "seq"),
        P("fsdp"),
        P("fsdp", None),
        P("fsdp"),
    )
    out_specs = P("fsdp", None, "seq")
    return jax.shard_map(body, mesh=mesh, in_specs=in_specs, out_specs=out_specs, check_vma=False)
```
